256 devices in a mesh: shot: 8 (over y, core), band: 32 (over x, z).
Axes of the slice: x: 4, y: 4, z: 8, core: 2. Of those that a mesh axis runs over, the one named last changes fastest.
Arguments:
- sensitivity: bfloat16 [16384, 128, 128], P(('shot', 'band')), may hold values from -0.0625 to 0.0625
- bundle_of: int32 [16384], P(('shot', 'band')), may hold values from 0 to 31
- cellblock_of: int32 [16384], P(('shot', 'band')), may hold values from 0 to 15
- state: float32 [65536, 128], P('band'), may hold values from -6 to 6
- prior_velocity: float32 [65536, 128], P('band'), may hold values from -6 to 6
- observed: float32 [256, 128], P(('shot', 'band')), may hold values from -6 to 6
- pick_weight: float32 [256, 128], P(('shot', 'band')), may hold values from 0.3 to 3
Outputs:
- new_state: float32 [65536, 128], P('band')
- weighted_residual: float32 [256, 128, 128], P(('shot', 'band'))
The draws below stay inside these ranges and needn't reach their ends.
Inputs may be any that keep to these rules, and one draw needn't show every extreme that they name: bundle_of names a bundle of the block's own source group. cellblock_of names a cell block of the block's own depth band.
All inputs are finite; a program needn't handle non-finite values.
Results may differ from the reference program's by a relative error of at most 0.0059.
Values may be sent and summed in bfloat16 or wider, within the bound.
A program may use at most 64 MiB of HBM per device.

```python
import math
import jax
import jax.numpy as jnp
from jax import lax

RAYS = 128
CBLK = 128
SAMPLES = 128
NBLK = 64
CB_DEV = 16
BUNDLES = 32
CELLS = 65536
N_SHOT = 8
N_BAND = 32


def touch_ends(drawn, own_key, least, high):
    place = [jax.random.randint(jax.random.fold_in(own_key, axis), (), 0, length) for axis, length in enumerate(drawn.shape)]
    longest = drawn.shape.index(max(drawn.shape))
    next_to = place[:longest] + [(place[longest] + 1) % drawn.shape[longest]] + place[longest + 1:]
    return drawn.at[tuple(place)].set(least).at[tuple(next_to)].set(high)


def steps_of(own_key, dims, split, smallest, top_value):
    def one(dim, shards_of):
        heights = jax.random.uniform(jax.random.fold_in(jax.random.fold_in(own_key, 6), dim), (shards_of,), jnp.float32, smallest / len(split), top_value / len(split))
        return jnp.repeat(jnp.exp(heights), dims[dim] // shards_of).reshape((-1,) + (1,) * (len(dims) - dim - 1))

    level = one(*split[0])
    for cut in split[1:]:
        level = level * one(*cut)
    return level


def gaussian(stream_key, dims, deviation, bound, split=(), dtype=jnp.bfloat16):
    array = jax.random.normal(stream_key, dims, jnp.float32) * deviation
    if len(split) > 0:
        array = steps_of(stream_key, dims, split, -0.22, 0.18) * array
    return jnp.clip(array, min=-bound, max=bound).astype(dtype)


def setup_inputs(seed: int = 0) -> dict:
    seeds = jax.random.split(jax.random.key(seed), 8)
    sensitivity = gaussian(seeds[0], (N_SHOT * N_BAND * NBLK, RAYS, CBLK), (CBLK * NBLK * N_BAND // BUNDLES) ** -0.5, 0.0625, ((0, 256),))
    bundle_of = touch_ends(jax.random.randint(seeds[1], (N_SHOT * N_BAND * NBLK,), 0, BUNDLES), jax.random.fold_in(seeds[1], 1), 0, BUNDLES - 1).astype(jnp.int32)
    cellblock_of = touch_ends(jax.random.randint(seeds[2], (N_SHOT * N_BAND * NBLK,), 0, CB_DEV), jax.random.fold_in(seeds[2], 1), 0, CB_DEV - 1).astype(jnp.int32)
    state = gaussian(seeds[3], (CELLS, SAMPLES), 1.0, 6.0, ((0, 32),), jnp.float32)
    prior_velocity = gaussian(seeds[4], (CELLS, SAMPLES), 1.0, 6.0, ((0, 32),), jnp.float32)
    observed = gaussian(seeds[5], (N_SHOT * BUNDLES, RAYS), 1.0, 6.0, ((0, 256),), jnp.float32)
    pick_weight = jnp.clip(jnp.exp(math.log(3.0) - 2.3025851 * jax.random.uniform(seeds[6], (N_SHOT * BUNDLES, RAYS), jnp.float32) ** steps_of(seeds[6], (N_SHOT * BUNDLES, RAYS), ((0, 256),), -0.2, 0.2)), 0.3, 3.0)
    return dict(sensitivity=sensitivity, bundle_of=bundle_of, cellblock_of=cellblock_of, state=state, prior_velocity=prior_velocity, observed=observed, pick_weight=pick_weight)


def forward(sens, bund, cblk, probe):
    def per_shot(shot_index):
        def step(acc, band_index):
            columns = probe[band_index][cblk[shot_index, band_index]]
            prod = jnp.einsum('krc,kce->kre', sens[shot_index, band_index].astype(jnp.float32), columns.astype(jnp.float32))
            return acc + jax.ops.segment_sum(prod, bund[shot_index, band_index], num_segments=BUNDLES), None
        start = jnp.zeros((BUNDLES, RAYS, SAMPLES), jnp.float32)
        acc, _ = lax.scan(step, start, jnp.arange(N_BAND))
        return acc
    return lax.map(per_shot, jnp.arange(N_SHOT))


def adjoint(sens, bund, cblk, resid):
    def per_band(band_index):
        def step(acc, shot_index):
            rows = resid[shot_index][bund[shot_index, band_index]]
            contrib = jnp.einsum('krc,kre->kce', sens[shot_index, band_index].astype(jnp.float32), rows.astype(jnp.float32))
            return acc + jax.ops.segment_sum(contrib, cblk[shot_index, band_index], num_segments=CB_DEV), None
        start = jnp.zeros((CB_DEV, CBLK, SAMPLES), jnp.float32)
        acc, _ = lax.scan(step, start, jnp.arange(N_SHOT))
        return acc
    return lax.map(per_band, jnp.arange(N_BAND)).reshape(CELLS, SAMPLES)


def reference(sensitivity, bundle_of, cellblock_of, state, prior_velocity, observed, pick_weight):
    sens = sensitivity.reshape(N_SHOT, N_BAND, NBLK, RAYS, CBLK)
    bund = bundle_of.reshape(N_SHOT, N_BAND, NBLK)
    cblk = cellblock_of.reshape(N_SHOT, N_BAND, NBLK)
    obs = observed.reshape(N_SHOT, BUNDLES, RAYS)[..., None]
    wts = pick_weight.reshape(N_SHOT, BUNDLES, RAYS)[..., None]
    probe1 = (state + 0.5 * prior_velocity).astype(jnp.bfloat16).reshape(N_BAND, CB_DEV, CBLK, SAMPLES)
    res1 = wts * (forward(sens, bund, cblk, probe1) - obs)
    grad1 = adjoint(sens, bund, cblk, res1.astype(jnp.bfloat16))
    middle = state + 0.5 * (prior_velocity - 0.5 * grad1)
    probe2 = (middle + 0.5 * prior_velocity).astype(jnp.bfloat16).reshape(N_BAND, CB_DEV, CBLK, SAMPLES)
    res2 = wts * (forward(sens, bund, cblk, probe2) - obs)
    grad2 = adjoint(sens, bund, cblk, res2.astype(jnp.bfloat16))
    new_state = state + 0.5 * (prior_velocity - 0.25 * (grad1 + grad2))
    return new_state, res2.reshape(N_SHOT * BUNDLES, RAYS, SAMPLES)
```

```python
import functools

import jax
import jax.numpy as jnp
from jax import lax
from jax.experimental import pallas as pl
from jax.experimental.pallas import tpu as pltpu
from jax.sharding import PartitionSpec as P

MESH = pl.DeviceIdType.MESH
BF16 = jnp.bfloat16
F32 = jnp.float32
I32 = jnp.int32
T = 128
NT_DIMS = (((1,), (1,)), ((), ()))
NN_DIMS = (((1,), (0,)), ((), ()))
UNROLL = 32
GROUPS = ((0, ((16, True), (48, False))), (64, ((16, True), (48, False))))
ORD_F, CEL_F, KEEP_F, LAST_F, ORD_A, BX_A, BZ_A, KEEP_A, LAST_A = range(9)


def band_grid(nband):
    nx = 4 if nband >= 16 else 2
    return nx, nband // nx


class Plan:
    def __init__(self, nshot, nband, nblk, ncell, groups):
        self.nx, self.nz = band_grid(nband)
        self.ns = nshot
        self.nblk, self.ncell, self.nband = nblk, ncell, nband
        self.cown = ncell // nshot
        self.groups = groups
        self.nsem = len(groups) * 2 * 2 + sum(8 * len(parts) for _, parts in groups)


def group_buffers(pn):
    bufs = {}
    for g, (row, parts) in enumerate(pn.groups):
        m = sum(rows for rows, _ in parts)
        bufs[f"pref{g}"] = ((pn.nblk + 1, m, T), F32)
        bufs[f"g1_{g}"] = ((pn.cown, m, T), F32)
        for p in range(2):
            bufs[f"Q{g}_{p}"] = ((pn.ncell, m, T), BF16)
            for d in "sr":
                bufs[f"y{d}{g}_{p}"] = ((pn.ns - 1, pn.cown, m, T), BF16)
            for u, (rows, zfirst) in enumerate(parts):
                first, second = (pn.nz, pn.nx) if zfirst else (pn.nx, pn.nz)
                k = f"{g}_{p}_{u}"
                bufs[f"acc{k}"] = ((second, rows, T), F32)
                bufs[f"R{k}"] = ((first, second, rows, T), BF16)
                for d in "sr":
                    bufs[f"a{d}{k}"] = ((first - 1, second, rows, T), BF16)
                    bufs[f"b{d}{k}"] = ((second - 1, rows, T), BF16)
    return bufs


def index_table(bun_ref, cel_ref, pad_ref, table_ref, pn):
    n = pn.nblk
    lane = lax.broadcasted_iota(I32, (T, T), 1)
    sub = lax.broadcasted_iota(I32, (T, T), 0)
    pad_ref[...] = jnp.full(pad_ref.shape, 127, I32)
    pad_ref[0:1, 0:n] = bun_ref[...].reshape(1, n)
    pad_ref[8:9, 0:n] = cel_ref[...].reshape(1, n)
    b = jnp.broadcast_to(pad_ref[0:1, :], (T, T))
    c = jnp.broadcast_to(pad_ref[8:9, :], (T, T))

    def ranked(key, other):
        key_t = key.T
        before = (key_t < key) | ((key_t == key) & (sub < lane))
        rank = jnp.sum(before.astype(I32), axis=0, keepdims=True)
        same = jnp.sum(((key_t == key) & (sub < lane)).astype(I32), axis=0, keepdims=True)
        keep = (same > 0).astype(I32)
        packed = rank * 65536 + keep * 16384 + other[0:1, :] * 128 + lane[0:1, :]
        packed = jnp.broadcast_to(packed, (T, T)).T
        mine = (packed // 65536) == lane
        row = jnp.sum(jnp.where(mine, packed % 65536, 0), axis=0, keepdims=True)
        upto = jnp.sum((key_t <= lane).astype(I32), axis=0, keepdims=True)
        held = jnp.sum((key_t == lane).astype(I32), axis=0, keepdims=True)
        last = jnp.where(held > 0, upto - 1, n)
        return row % 128, (row // 128) % 128, row // 16384, last

    order, other, keep, last = ranked(b, c)
    table_ref[ORD_F : ORD_F + 1, :] = order
    table_ref[CEL_F : CEL_F + 1, :] = other
    table_ref[KEEP_F : KEEP_F + 1, :] = keep
    table_ref[LAST_F : LAST_F + 1, :] = last
    order, other, keep, last = ranked(c, b)
    table_ref[ORD_A : ORD_A + 1, :] = order
    table_ref[BX_A : BX_A + 1, :] = other // pn.nz
    table_ref[BZ_A : BZ_A + 1, :] = other % pn.nz
    table_ref[KEEP_A : KEEP_A + 1, :] = keep
    table_ref[LAST_A : LAST_A + 1, :] = last


def kernel(pn, names, sens_hbm, bun_ref, cel_ref, state_hbm, prior_hbm, obs_ref, wgt_ref, new_ref, res_ref, *scratch):
    w = dict(zip(names, scratch))
    sens, state, prior = w["sens"], w["state"], w["prior"]
    tab, x1, res_t = w["tab"], w["x1"], w["res_t"]
    st_t, pr_t = w["st_t"], w["pr_t"]
    load_sem, send_sem, recv_sem = w["load_sem"], w["send_sem"], w["recv_sem"]
    nx, nz, ns, nblk, ncell, cown = pn.nx, pn.nz, pn.ns, pn.nblk, pn.ncell, pn.cown

    s, b = lax.axis_index("shot"), lax.axis_index("band")
    x, z = b // nz, b % nz
    size = {"x": nx, "s": ns, "z": nz}
    place = {"x": x, "s": s, "z": z}

    def at(axis, k):
        return (place[axis] + k) % size[axis]

    def device(axis, k):
        if axis == "x":
            return {"band": at("x", k) * nz + z}
        if axis == "z":
            return {"band": x * nz + at("z", k)}
        return {"shot": at("s", k)}

    def order(axis):
        n = size[axis]
        return sorted(range(1, n), key=lambda k: -min(k, n - k))

    load_state = pltpu.make_async_copy(state_hbm, state, load_sem.at[0])
    load_prior = pltpu.make_async_copy(prior_hbm, prior, load_sem.at[1])
    load_sens = pltpu.make_async_copy(sens_hbm, sens, load_sem.at[2])
    load_state.start()
    load_prior.start()
    load_sens.start()

    barrier = pltpu.get_barrier_semaphore()
    greet = [(axis, k) for axis in "xzs" for k in order(axis)]
    for axis, k in greet:
        pl.semaphore_signal(barrier, inc=1, device_id=device(axis, k), device_id_type=MESH)

    index_table(bun_ref, cel_ref, w["pad"], w["table"], pn)
    to_smem = pltpu.make_async_copy(w["table"], tab, load_sem.at[3])
    to_smem.start()

    load_state.wait()
    load_prior.wait()

    def probe_block(i, carry):
        x1[i] = (state[i] + 0.5 * prior[i]).astype(BF16).T
        return carry

    lax.fori_loop(0, ncell, probe_block, 0, unroll=4)
    for g in range(len(pn.groups)):
        w[f"pref{g}"][nblk] = jnp.zeros(w[f"pref{g}"].shape[1:], F32)
    to_smem.wait()
    load_sens.wait()

    counter = [0]
    sent = []
    first_send = [True]

    class Exchange:
        def __init__(self, axis, src_of, dst_of, send_all, recv_all):
            self.index = counter[0]
            counter[0] += 1
            self.recv_all = recv_all
            sent.append((self.index, send_all))
            if first_send[0]:
                first_send[0] = False
                pl.semaphore_wait(barrier, len(greet))
            for k in order(axis):
                pltpu.make_async_remote_copy(
                    src_ref=src_of(k), dst_ref=dst_of(k), send_sem=send_sem.at[self.index],
                    recv_sem=recv_sem.at[self.index], device_id=device(axis, k), device_id_type=MESH).start()

        def wait(self):
            pltpu.make_async_copy(self.recv_all, self.recv_all, recv_sem.at[self.index]).wait()

    def scatter(axis, fill, sbuf, rbuf):
        for k in order(axis):
            fill(at(axis, k), sbuf.at[k - 1])
        return Exchange(axis, lambda k: sbuf.at[k - 1], lambda k: rbuf.at[k - 1], sbuf, rbuf)

    def gather(axis, ref, chunk, n):
        mine = ref.at[pl.ds(place[axis] * chunk, chunk)]
        rest = ref.at[pl.ds(0, (n - 1) * chunk)]
        return Exchange(axis, lambda k: mine, lambda k: mine, rest, rest)

    def products(pref, m, order_row, keep_row, dims, field):
        def step(k, acc):
            prod = lax.dot_general(field(k), sens[tab[order_row, k]], dims, preferred_element_type=F32)
            acc = jnp.where(tab[keep_row, k] > 0, acc, 0.0) + prod
            pref[k] = acc
            return acc

        lax.fori_loop(0, nblk, step, jnp.zeros((m, T), F32), unroll=UNROLL)

    def group(g):
        row, parts = pn.groups[g]
        m = sum(rows for rows, _ in parts)
        starts = [sum(rows for rows, _ in parts[:u]) for u in range(len(parts))]
        pref, g1 = w[f"pref{g}"], w[f"g1_{g}"]
        span = slice(row, row + m)
        for p in range(2):
            Q = w[f"Q{g}_{p}"]
            ys, yr = w[f"ys{g}_{p}"], w[f"yr{g}_{p}"]

            def field_f(k):
                i = tab[CEL_F, k]
                return x1[i, span, :] if p == 0 else w[f"Q{g}_0"][i]

            products(pref, m, ORD_F, KEEP_F, NT_DIMS, field_f)

            def part(u):
                rows, zfirst = parts[u]
                key = f"{g}_{p}_{u}"
                asb, arb, bsb, brb = (w[q + key] for q in ("as", "ar", "bs", "br"))
                acc, R = w["acc" + key], w["R" + key]
                inner = slice(starts[u], starts[u] + rows)
                one, two = ("z", "x") if zfirst else ("x", "z")
                first, second = size[one], size[two]

                def term(d, c):
                    bundle = c * nz + d if zfirst else d * nz + c
                    return pref[tab[LAST_F, bundle], inner, :]

                def fill_one(d, ref):
                    for c in range(second):
                        ref[c] = term(d, c).astype(BF16)

                ex = scatter(one, fill_one, asb, arb)
                yield
                ex.wait()
                for c in range(second):
                    total = term(place[one], c)
                    for k in range(1, first):
                        total = total + arb[k - 1, c].astype(F32)
                    acc[c] = total

                def fill_two(d, ref):
                    ref[...] = acc[d].astype(BF16)

                ex = scatter(two, fill_two, bsb, brb)
                yield
                ex.wait()
                pred = acc[place[two]]
                for k in range(1, second):
                    pred = pred + brb[k - 1].astype(F32)
                r = wgt_ref[...] * (pred - obs_ref[...])
                if p == 1:
                    res_t[row + starts[u] : row + starts[u] + rows, :] = r
                R[place[one], place[two]] = r.astype(BF16)
                ex = gather(two, R.at[place[one]], 1, second)
                yield
                ex.wait()
                ex = gather(one, R, 1, first)
                yield
                ex.wait()

            running = [part(u) for u in range(len(parts))]
            for _ in range(4):
                for q in running:
                    next(q)
                yield
            for q in running:
                for _ in q:
                    pass

            def field_a(k):
                bx, bz = tab[BX_A, k], tab[BZ_A, k]
                pieces = []
                for u, (rows, zfirst) in enumerate(parts):
                    R = w[f"R{g}_{p}_{u}"]
                    pieces.append(R[bz, bx] if zfirst else R[bx, bz])
                return pieces[0] if len(pieces) == 1 else jnp.concatenate(pieces, axis=0)

            products(pref, m, ORD_A, KEEP_A, NN_DIMS, field_a)

            def grad_term(d, c):
                return pref[tab[LAST_A, d * cown + c]]

            def fill_grad(d, ref):
                for c in range(cown):
                    ref[c] = grad_term(d, c).astype(BF16)

            ex = scatter("s", fill_grad, ys, yr)
            if g == 0 and p == 0:
                for c in range(cown):
                    st_t[c] = state[s * cown + c].T
                    pr_t[c] = prior[s * cown + c].T
            yield
            ex.wait()
            for c in range(cown):
                grad = grad_term(s, c)
                for k in range(1, ns):
                    grad = grad + yr[k - 1, c].astype(F32)
                if p == 0:
                    g1[c] = grad
                    st, pr = st_t[c, span, :], pr_t[c, span, :]
                    middle = st + 0.5 * (pr - 0.5 * grad)
                    Q[s * cown + c] = (middle + 0.5 * pr).astype(BF16)
                else:
                    Q[s * cown + c] = (g1[c] + grad).astype(BF16)
            ex = gather("s", Q, cown, ns)
            yield
            ex.wait()

    live = [group(g) for g in range(len(pn.groups))]
    while live:
        for q in list(live):
            try:
                next(q)
            except StopIteration:
                live.remove(q)

    res_ref[0] = res_t[...].T

    def final_block(i, carry):
        pieces = [w[f"Q{g}_1"][i].astype(F32) for g in range(len(pn.groups))]
        total = jnp.concatenate(pieces, axis=0).T
        new_ref[i] = state[i] + 0.5 * (prior[i] - 0.25 * total)
        return carry

    lax.fori_loop(0, ncell, final_block, 0, unroll=4)
    for index, ref in sent:
        pltpu.make_async_copy(ref, ref, send_sem.at[index]).wait()


def per_device(pn, sensitivity, bundle_of, cellblock_of, state, prior_velocity, observed, pick_weight):
    ncell, nblk = pn.ncell, pn.nblk
    bufs = {
        "sens": ((nblk, T, T), BF16),
        "state": ((ncell, T, T), F32),
        "prior": ((ncell, T, T), F32),
        "x1": ((ncell, T, T), BF16),
        "res_t": ((T, T), F32),
        "st_t": ((pn.cown, T, T), F32),
        "pr_t": ((pn.cown, T, T), F32),
        "pad": ((16, T), I32),
        "table": ((16, T), I32),
    }
    bufs.update(group_buffers(pn))
    shapes = {k: pltpu.VMEM(*v) for k, v in bufs.items()}
    shapes["tab"] = pltpu.SMEM((16, T), I32)
    shapes["load_sem"] = pltpu.SemaphoreType.DMA((4,))
    shapes["send_sem"] = pltpu.SemaphoreType.DMA((pn.nsem,))
    shapes["recv_sem"] = pltpu.SemaphoreType.DMA((pn.nsem,))
    hbm = pl.BlockSpec(memory_space=pl.ANY)
    vmem = pl.BlockSpec(memory_space=pltpu.VMEM)
    new_state, res = pl.pallas_call(
        functools.partial(kernel, pn, list(shapes)),
        out_shape=(
            jax.ShapeDtypeStruct((ncell, T, T), F32),
            jax.ShapeDtypeStruct((1, T, T), F32),
        ),
        in_specs=[hbm, vmem, vmem, hbm, hbm, vmem, vmem],
        out_specs=(vmem, vmem),
        scratch_shapes=list(shapes.values()),
        compiler_params=pltpu.CompilerParams(
            collective_id=0, has_side_effects=True, vmem_limit_bytes=60 * 1024 * 1024),
        name="guided_update",
    )(sensitivity, bundle_of, cellblock_of, state.reshape(ncell, T, T), prior_velocity.reshape(ncell, T, T),
      observed, pick_weight)
    return new_state.reshape(ncell * T, T), res


def solution(mesh):
    nshot, nband = mesh.shape["shot"], mesh.shape["band"]
    in_specs = (
        P(("shot", "band"), None, None),
        P(("shot", "band")),
        P(("shot", "band")),
        P("band", None),
        P("band", None),
        P(("shot", "band"), None),
        P(("shot", "band"), None),
    )
    out_specs = (P("band", None), P(("shot", "band"), None, None))

    def body(sensitivity, bundle_of, cellblock_of, state, *rest):
        pn = Plan(nshot, nband, sensitivity.shape[0], state.shape[0] // T,
                  GROUPS)
        return per_device(pn, sensitivity, bundle_of, cellblock_of, state, *rest)

    return jax.shard_map(body, mesh=mesh, in_specs=in_specs, out_specs=out_specs, check_vma=False)
```

```python
import functools

import jax
import jax.numpy as jnp
from jax import lax
from jax.experimental import pallas as pl
from jax.experimental.pallas import tpu as pltpu
from jax.sharding import PartitionSpec as P

MESH = pl.DeviceIdType.MESH
BF16 = jnp.bfloat16
F32 = jnp.float32
I32 = jnp.int32
T = 128
NT_DIMS = (((1,), (1,)), ((), ()))
NN_DIMS = (((1,), (0,)), ((), ()))
UNROLL = 32
LAG = 0
VMEM_MB = 60
GROUPS = ((0, ((32, False),)), (32, ((16, True), (32, False))), (80, ((16, True), (32, False))))
ORD_F, CEL_F, KEEP_F, LAST_F, ORD_A, BX_A, BZ_A, KEEP_A, LAST_A, RX_A, RZ_A = range(11)


def band_grid(nband):
    nx = 4 if nband >= 16 else 2
    return nx, nband // nx


class Plan:
    def __init__(self, nshot, nband, nblk, ncell, groups):
        self.nx, self.nz = band_grid(nband)
        self.ny = nshot // 2
        self.nblk, self.ncell, self.nband = nblk, ncell, nband
        self.half = ncell // 2
        self.cown = ncell // nshot
        self.groups = groups
        self.nsem = len(groups) * 2 * 4 + sum(14 * len(parts) for _, parts in groups)


def spans(n):
    far = max(n // 2 - 1, 0)
    return [(0, n - far)] + ([(n - far, far)] if far else [])


def group_buffers(pn):
    bufs = {}
    for g, (row, parts) in enumerate(pn.groups):
        m = sum(rows for rows, _ in parts)
        bufs[f"pref{g}"] = ((pn.nblk + 1, m, T), F32)
        bufs[f"g1_{g}"] = ((pn.cown, m, T), F32)
        for p in range(2):
            bufs[f"Q{g}_{p}"] = ((pn.ncell, m, T), BF16)
            for d in "sr":
                bufs[f"c{d}{g}_{p}"] = ((pn.half, m, T), BF16)
                bufs[f"y{d}{g}_{p}"] = ((max(pn.ny - 1, 1), pn.cown, m, T), BF16)
            for u, (rows, zfirst) in enumerate(parts):
                first, second = (pn.nz, pn.nx) if zfirst else (pn.nx, pn.nz)
                k = f"{g}_{p}_{u}"
                bufs[f"own{k}"] = ((rows, T), F32)
                bufs[f"R{k}"] = ((first, second, rows, T), BF16)
                for d in "sr":
                    for q, (_, count) in enumerate(spans(second)):
                        bufs[f"a{d}{q}{k}"] = ((first - 1, count, rows, T), BF16)
                    bufs[f"b{d}{k}"] = ((second - 1, rows, T), BF16)
    return bufs


def index_table(bun_ref, cel_ref, pad_ref, table_ref, pn, x, z):
    n = pn.nblk
    lane = lax.broadcasted_iota(I32, (T, T), 1)
    sub = lax.broadcasted_iota(I32, (T, T), 0)
    pad_ref[...] = jnp.full(pad_ref.shape, 127, I32)
    pad_ref[0:1, 0:n] = bun_ref[...].reshape(1, n)
    pad_ref[8:9, 0:n] = cel_ref[...].reshape(1, n)
    b = jnp.broadcast_to(pad_ref[0:1, :], (T, T))
    c = jnp.broadcast_to(pad_ref[8:9, :], (T, T))

    def ranked(key, other):
        key_t = key.T
        before = (key_t < key) | ((key_t == key) & (sub < lane))
        rank = jnp.sum(before.astype(I32), axis=0, keepdims=True)
        same = jnp.sum(((key_t == key) & (sub < lane)).astype(I32), axis=0, keepdims=True)
        keep = (same > 0).astype(I32)
        packed = rank * 65536 + keep * 16384 + other[0:1, :] * 128 + lane[0:1, :]
        packed = jnp.broadcast_to(packed, (T, T)).T
        mine = (packed // 65536) == lane
        row = jnp.sum(jnp.where(mine, packed % 65536, 0), axis=0, keepdims=True)
        upto = jnp.sum((key_t <= lane).astype(I32), axis=0, keepdims=True)
        held = jnp.sum((key_t == lane).astype(I32), axis=0, keepdims=True)
        last = jnp.where(held > 0, upto - 1, n)
        return row % 128, (row // 128) % 128, row // 16384, last

    order, other, keep, last = ranked(b, c)
    table_ref[ORD_F : ORD_F + 1, :] = order
    table_ref[CEL_F : CEL_F + 1, :] = other
    table_ref[KEEP_F : KEEP_F + 1, :] = keep
    table_ref[LAST_F : LAST_F + 1, :] = last
    order, other, keep, last = ranked(c, b)
    table_ref[ORD_A : ORD_A + 1, :] = order
    table_ref[BX_A : BX_A + 1, :] = other // pn.nz
    table_ref[BZ_A : BZ_A + 1, :] = other % pn.nz
    table_ref[RX_A : RX_A + 1, :] = (other // pn.nz + (pn.nx + pn.nx // 4 - x)) % pn.nx
    table_ref[RZ_A : RZ_A + 1, :] = (other % pn.nz + (pn.nz + pn.nz // 4 - z)) % pn.nz
    table_ref[KEEP_A : KEEP_A + 1, :] = keep
    table_ref[LAST_A : LAST_A + 1, :] = last


def kernel(pn, names, sens_hbm, bun_hbm, cel_hbm, state_hbm, prior_hbm, obs_hbm, wgt_hbm, new_ref, res_ref, *scratch):
    w = dict(zip(names, scratch))
    sens, state, prior = w["sens"], w["state"], w["prior"]
    tab, x1, res_t = w["tab"], w["x1"], w["res_t"]
    st_t, pr_t = w["st_t"], w["pr_t"]
    load_sem, send_sem, recv_sem = w["load_sem"], w["send_sem"], w["recv_sem"]
    nx, nz, ny, nblk, ncell, half, cown = pn.nx, pn.nz, pn.ny, pn.nblk, pn.ncell, pn.half, pn.cown

    s, b = lax.axis_index("shot"), lax.axis_index("band")
    y, core = s // 2, s % 2
    x, z = b // nz, b % nz
    size = {"x": nx, "y": ny, "z": nz, "core": 2}
    place = {"x": x, "y": y, "z": z, "core": core}

    def at(axis, k):
        return (place[axis] + k) % size[axis]

    def device(axis, k):
        if axis == "x":
            return {"band": at("x", k) * nz + z}
        if axis == "z":
            return {"band": x * nz + at("z", k)}
        if axis == "y":
            return {"shot": at("y", k) * 2 + core}
        return {"shot": y * 2 + (1 - core)}

    def order(axis):
        n = size[axis]
        return sorted(range(1, n), key=lambda k: -min(k, n - k))

    small = []
    for q, (src, name) in enumerate(((bun_hbm, "bun"), (cel_hbm, "cel"), (obs_hbm, "obs"), (wgt_hbm, "wgt"))):
        small.append(pltpu.make_async_copy(src, w[name], load_sem.at[4 + q]))
        small[-1].start()
    obs_ref, wgt_ref = w["obs"], w["wgt"]
    load_state = pltpu.make_async_copy(state_hbm, state, load_sem.at[0])
    load_prior = pltpu.make_async_copy(prior_hbm, prior, load_sem.at[1])
    load_sens = pltpu.make_async_copy(sens_hbm, sens, load_sem.at[2])
    load_state.start()
    load_prior.start()
    load_sens.start()

    barrier = pltpu.get_barrier_semaphore()
    greet = [(axis, k) for axis in ("z", "x", "y", "core") for k in order(axis)]
    for axis, k in greet:
        pl.semaphore_signal(barrier, inc=1, device_id=device(axis, k), device_id_type=MESH)

    for load in small:
        load.wait()
    index_table(w["bun"], w["cel"], w["pad"], w["table"], pn, x, z)
    to_smem = pltpu.make_async_copy(w["table"], tab, load_sem.at[3])
    to_smem.start()

    load_state.wait()
    load_prior.wait()

    def probe_block(i, carry):
        x1[i] = (state[i] + 0.5 * prior[i]).astype(BF16).T
        return carry

    lax.fori_loop(0, ncell, probe_block, 0, unroll=4)
    for g in range(len(pn.groups)):
        w[f"pref{g}"][nblk] = jnp.zeros(w[f"pref{g}"].shape[1:], F32)
    to_smem.wait()
    load_sens.wait()

    counter = [0]
    sent = []
    first_send = [True]

    class Exchange:
        def __init__(self, axis, sent_all, came_all):
            self.axis, self.came_all = axis, came_all
            self.index = counter[0]
            counter[0] += 1
            sent.append((self.index, sent_all))
            if first_send[0]:
                first_send[0] = False
                pl.semaphore_wait(barrier, len(greet))

        def send(self, k, src, dst):
            pltpu.make_async_remote_copy(
                src_ref=src, dst_ref=dst, send_sem=send_sem.at[self.index], recv_sem=recv_sem.at[self.index],
                device_id=device(self.axis, k), device_id_type=MESH).start()

        def wait(self):
            pltpu.make_async_copy(self.came_all, self.came_all, recv_sem.at[self.index]).wait()

    def products(pref, m, order_row, keep_row, dims, field):
        def step(k, acc):
            prod = lax.dot_general(field(k), sens[tab[order_row, k]], dims, preferred_element_type=F32)
            acc = jnp.where(tab[keep_row, k] > 0, acc, 0.0) + prod
            pref[k] = acc
            return acc

        lax.fori_loop(0, nblk, step, jnp.zeros((m, T), F32), unroll=UNROLL)

    def group(g):
        row, parts = pn.groups[g]
        m = sum(rows for rows, _ in parts)
        starts = [sum(rows for rows, _ in parts[:u]) for u in range(len(parts))]
        pref, g1 = w[f"pref{g}"], w[f"g1_{g}"]
        span = slice(row, row + m)
        for p in range(2):
            Q = w[f"Q{g}_{p}"]
            ys, yr = w[f"ys{g}_{p}"], w[f"yr{g}_{p}"]

            def field_f(k):
                i = tab[CEL_F, k]
                return x1[i, span, :] if p == 0 else w[f"Q{g}_0"][i]

            products(pref, m, ORD_F, KEEP_F, NT_DIMS, field_f)

            def part(u):
                rows, zfirst = parts[u]
                key = f"{g}_{p}_{u}"
                bsb, brb, own, R = (w[q + key] for q in ("bs", "br", "own", "R"))
                inner = slice(starts[u], starts[u] + rows)
                one, two = ("z", "x") if zfirst else ("x", "z")
                first, second = size[one], size[two]
                back = second // 4
                mine = place[one]

                def term(d, c):
                    bundle = c * nz + d if zfirst else d * nz + c
                    return pref[tab[LAST_F, bundle], inner, :]

                opened = []
                for q, (low, count) in reversed(list(enumerate(spans(second)))):
                    asb, arb = w[f"as{q}" + key], w[f"ar{q}" + key]
                    ex = Exchange(one, asb, arb)
                    for k in order(one):
                        for j in range(count):
                            asb[k - 1, j] = term(at(one, k), at(two, low + j - back + second)).astype(BF16)
                        ex.send(k, asb.at[k - 1], arb.at[k - 1])
                    opened.append((ex, arb, low, count))
                yield
                across = Exchange(two, bsb, brb)
                for ex, arb, low, count in opened:
                    ex.wait()
                    for j in range(count):
                        k2 = (low + j - back) % second
                        total = term(mine, at(two, k2))
                        for k in range(1, first):
                            total = total + arb[k - 1, j].astype(F32)
                        if k2 == 0:
                            own[...] = total
                        else:
                            bsb[k2 - 1] = total.astype(BF16)
                            across.send(k2, bsb.at[k2 - 1], brb.at[k2 - 1])
                yield
                across.wait()
                pred = own[...]
                for k in range(1, second):
                    pred = pred + brb[k - 1].astype(F32)
                r = wgt_ref[...] * (pred - obs_ref[...])
                if p == 1:
                    res_t[row + starts[u] : row + starts[u] + rows, :] = r
                R[mine, back] = r.astype(BF16)
                opened = []
                for low, count in reversed(spans(second)):
                    steps = [(low + j - back) % second for j in range(count)]
                    steps = [k for k in steps if k]
                    every = R.at[0, pl.ds(0, len(steps))]
                    ex = Exchange(two, every, every)
                    for k in steps:
                        ex.send(k, R.at[mine, back], R.at[mine, (back - k) % second])
                    opened.append((ex, low, count))
                yield
                across = []
                for ex, low, count in reversed(opened):
                    ex.wait()
                    every = R.at[pl.ds(0, first - 1), pl.ds(0, count)]
                    out = Exchange(one, every, every)
                    ref = R.at[mine, pl.ds(low, count)]
                    for k in order(one):
                        out.send(k, ref, ref)
                    across.append(out)
                yield
                for out in across:
                    out.wait()

            running = [part(u) for u in range(len(parts))]
            for _ in range(4):
                for q in running:
                    next(q)
                yield
            for q in running:
                for _ in q:
                    pass

            def field_a(k):
                pieces = []
                for u, (rows, zfirst) in enumerate(parts):
                    R = w[f"R{g}_{p}_{u}"]
                    pieces.append(R[tab[BZ_A, k], tab[RX_A, k]] if zfirst else R[tab[BX_A, k], tab[RZ_A, k]])
                return pieces[0] if len(pieces) == 1 else jnp.concatenate(pieces, axis=0)

            products(pref, m, ORD_A, KEEP_A, NN_DIMS, field_a)

            cs, cr = w[f"cs{g}_{p}"], w[f"cr{g}_{p}"]
            for i in range(half):
                cs[i] = pref[tab[LAST_A, (1 - core) * half + i]].astype(BF16)
            ex = Exchange("core", cs, cr)
            ex.send(1, cs, cr)
            if g == 0 and p == 0:
                for c in range(cown):
                    st_t[c] = state[core * half + y * cown + c].T
                    pr_t[c] = prior[core * half + y * cown + c].T
            yield
            ex.wait()

            def grad_term(d, c):
                i = d * cown + c
                return pref[tab[LAST_A, core * half + i]] + cr[i].astype(F32)

            if ny > 1:
                ex = Exchange("y", ys, yr)
                for k in order("y"):
                    for c in range(cown):
                        ys[k - 1, c] = grad_term(at("y", k), c).astype(BF16)
                    ex.send(k, ys.at[k - 1], yr.at[k - 1])
                yield
                ex.wait()
            base = core * half + y * cown
            for c in range(cown):
                grad = grad_term(y, c)
                for k in range(1, ny):
                    grad = grad + yr[k - 1, c].astype(F32)
                if p == 0:
                    g1[c] = grad
                    st, pr = st_t[c, span, :], pr_t[c, span, :]
                    middle = st + 0.5 * (pr - 0.5 * grad)
                    Q[base + c] = (middle + 0.5 * pr).astype(BF16)
                else:
                    Q[base + c] = (g1[c] + grad).astype(BF16)
            if ny > 1:
                rest = Q.at[pl.ds(0, (ny - 1) * cown)]
                ref = Q.at[pl.ds(base, cown)]
                ex = Exchange("y", rest, rest)
                for k in order("y"):
                    ex.send(k, ref, ref)
                yield
                ex.wait()
            ref = Q.at[pl.ds(core * half, half)]
            ex = Exchange("core", ref, ref)
            ex.send(1, ref, ref)
            if p == 1:
                last.append(ex)
                return
            yield
            ex.wait()

    last = []
    live = [(g * LAG, group(g)) for g in range(len(pn.groups))]
    tick = 0
    while live:
        for start, q in list(live):
            if tick >= start and next(q, "end") == "end":
                live.remove((start, q))
        tick += 1

    res_ref[0] = res_t[...].T

    def final_block(i, start):
        pieces = [w[f"Q{g}_1"][start + i].astype(F32) for g in range(len(pn.groups))]
        total = jnp.concatenate(pieces, axis=0).T
        new_ref[start + i] = state[start + i] + 0.5 * (prior[start + i] - 0.25 * total)
        return start

    lax.fori_loop(0, half, final_block, core * half, unroll=4)
    for ex in last:
        ex.wait()
    lax.fori_loop(0, half, final_block, (1 - core) * half, unroll=4)
    for index, ref in sent:
        pltpu.make_async_copy(ref, ref, send_sem.at[index]).wait()


def per_device(pn, sensitivity, bundle_of, cellblock_of, state, prior_velocity, observed, pick_weight):
    ncell, nblk = pn.ncell, pn.nblk
    bufs = {
        "sens": ((nblk, T, T), BF16),
        "state": ((ncell, T, T), F32),
        "prior": ((ncell, T, T), F32),
        "x1": ((ncell, T, T), BF16),
        "res_t": ((T, T), F32),
        "st_t": ((pn.cown, T, T), F32),
        "pr_t": ((pn.cown, T, T), F32),
        "bun": ((nblk,), I32),
        "cel": ((nblk,), I32),
        "obs": ((1, T), F32),
        "wgt": ((1, T), F32),
        "pad": ((16, T), I32),
        "table": ((16, T), I32),
    }
    bufs.update(group_buffers(pn))
    shapes = {k: pltpu.VMEM(*v) for k, v in bufs.items()}
    shapes["tab"] = pltpu.SMEM((16, T), I32)
    shapes["load_sem"] = pltpu.SemaphoreType.DMA((8,))
    shapes["send_sem"] = pltpu.SemaphoreType.DMA((pn.nsem,))
    shapes["recv_sem"] = pltpu.SemaphoreType.DMA((pn.nsem,))
    hbm = pl.BlockSpec(memory_space=pltpu.HBM)
    vmem = pl.BlockSpec(memory_space=pltpu.VMEM)
    new_state, res = pl.pallas_call(
        functools.partial(kernel, pn, list(shapes)),
        out_shape=(
            jax.ShapeDtypeStruct((ncell, T, T), F32),
            jax.ShapeDtypeStruct((1, T, T), F32),
        ),
        in_specs=[hbm] * 7,
        out_specs=(vmem, vmem),
        scratch_shapes=list(shapes.values()),
        compiler_params=pltpu.CompilerParams(
            collective_id=0, has_side_effects=True, vmem_limit_bytes=VMEM_MB * 1024 * 1024),
        name="guided_update",
    )(sensitivity, bundle_of, cellblock_of, state.reshape(ncell, T, T), prior_velocity.reshape(ncell, T, T),
      observed, pick_weight)
    return new_state.reshape(ncell * T, T), res


def solution(mesh):
    nshot, nband = mesh.shape["shot"], mesh.shape["band"]
    in_specs = (
        P(("shot", "band"), None, None),
        P(("shot", "band")),
        P(("shot", "band")),
        P("band", None),
        P("band", None),
        P(("shot", "band"), None),
        P(("shot", "band"), None),
    )
    out_specs = (P("band", None), P(("shot", "band"), None, None))

    def body(sensitivity, bundle_of, cellblock_of, state, *rest):
        pn = Plan(nshot, nband, sensitivity.shape[0], state.shape[0] // T,
                  GROUPS)
        return per_device(pn, sensitivity, bundle_of, cellblock_of, state, *rest)

    return jax.shard_map(body, mesh=mesh, in_specs=in_specs, out_specs=out_specs, check_vma=False)
```

```python
import functools

import jax
import jax.numpy as jnp
from jax import lax
from jax.experimental import pallas as pl
from jax.experimental.pallas import tpu as pltpu
from jax.sharding import PartitionSpec as P

MESH = pl.DeviceIdType.MESH
BF16 = jnp.bfloat16
F32 = jnp.float32
I32 = jnp.int32
T = 128
NT_DIMS = (((1,), (1,)), ((), ()))
NN_DIMS = (((1,), (0,)), ((), ()))
UNROLL = 64
LAG = 0
VMEM_MB = 60
GROUPS = ((0, ((32, False),)), (32, ((16, True), (32, False))), (80, ((16, True), (32, False))))
ORD_F, CEL_F, KEEP_F, LAST_F, ORD_A, BX_A, BZ_A, KEEP_A, LAST_A, RX_A, RZ_A = range(11)


def band_grid(nband):
    nx = 4 if nband >= 16 else 2
    return nx, nband // nx


class Plan:
    def __init__(self, nshot, nband, nblk, ncell, groups):
        self.nx, self.nz = band_grid(nband)
        self.ny = nshot // 2
        self.nblk, self.ncell, self.nband = nblk, ncell, nband
        self.half = ncell // 2
        self.cown = ncell // nshot
        self.groups = groups
        self.nsem = len(groups) * 2 * 4 + sum(14 * len(parts) for _, parts in groups)


def spans(n):
    far = max(n // 2 - 1, 0)
    return [(0, n - far)] + ([(n - far, far)] if far else [])


def group_buffers(pn):
    bufs = {}
    for g, (row, parts) in enumerate(pn.groups):
        m = sum(rows for rows, _ in parts)
        bufs[f"pref{g}"] = ((pn.nblk + 1, m, T), F32)
        bufs[f"g1_{g}"] = ((pn.cown, m, T), F32)
        for p in range(2):
            bufs[f"Q{g}_{p}"] = ((pn.ncell, m, T), BF16)
            for d in "sr":
                bufs[f"c{d}{g}_{p}"] = ((pn.half, m, T), BF16)
                bufs[f"y{d}{g}_{p}"] = ((max(pn.ny - 1, 1), pn.cown, m, T), BF16)
            for u, (rows, zfirst) in enumerate(parts):
                first, second = (pn.nz, pn.nx) if zfirst else (pn.nx, pn.nz)
                k = f"{g}_{p}_{u}"
                bufs[f"own{k}"] = ((rows, T), F32)
                bufs[f"R{k}"] = ((first, second, rows, T), BF16)
                for d in "sr":
                    for q, (_, count) in enumerate(spans(second)):
                        bufs[f"a{d}{q}{k}"] = ((first - 1, count, rows, T), BF16)
                    bufs[f"b{d}{k}"] = ((second - 1, rows, T), BF16)
    return bufs


def index_table(bun_ref, cel_ref, pad_ref, table_ref, pn, x, z):
    n = pn.nblk
    lane = lax.broadcasted_iota(I32, (T, T), 1)
    sub = lax.broadcasted_iota(I32, (T, T), 0)
    pad_ref[...] = jnp.full(pad_ref.shape, 127, I32)
    pad_ref[0:1, 0:n] = bun_ref[...].reshape(1, n)
    pad_ref[8:9, 0:n] = cel_ref[...].reshape(1, n)
    b = jnp.broadcast_to(pad_ref[0:1, :], (T, T))
    c = jnp.broadcast_to(pad_ref[8:9, :], (T, T))

    def ranked(key, other):
        key_t = key.T
        before = (key_t < key) | ((key_t == key) & (sub < lane))
        rank = jnp.sum(before.astype(I32), axis=0, keepdims=True)
        same = jnp.sum(((key_t == key) & (sub < lane)).astype(I32), axis=0, keepdims=True)
        keep = (same > 0).astype(I32)
        packed = rank * 65536 + keep * 16384 + other[0:1, :] * 128 + lane[0:1, :]
        packed = jnp.broadcast_to(packed, (T, T)).T
        mine = (packed // 65536) == lane
        row = jnp.sum(jnp.where(mine, packed % 65536, 0), axis=0, keepdims=True)
        upto = jnp.sum((key_t <= lane).astype(I32), axis=0, keepdims=True)
        held = jnp.sum((key_t == lane).astype(I32), axis=0, keepdims=True)
        last = jnp.where(held > 0, upto - 1, n)
        return row % 128, (row // 128) % 128, row // 16384, last

    order, other, keep, last = ranked(b, c)
    table_ref[ORD_F : ORD_F + 1, :] = order
    table_ref[CEL_F : CEL_F + 1, :] = other
    table_ref[KEEP_F : KEEP_F + 1, :] = keep
    table_ref[LAST_F : LAST_F + 1, :] = last
    order, other, keep, last = ranked(c, b)
    table_ref[ORD_A : ORD_A + 1, :] = order
    table_ref[BX_A : BX_A + 1, :] = other // pn.nz
    table_ref[BZ_A : BZ_A + 1, :] = other % pn.nz
    table_ref[RX_A : RX_A + 1, :] = (other // pn.nz + (pn.nx + pn.nx // 4 - x)) % pn.nx
    table_ref[RZ_A : RZ_A + 1, :] = (other % pn.nz + (pn.nz + pn.nz // 4 - z)) % pn.nz
    table_ref[KEEP_A : KEEP_A + 1, :] = keep
    table_ref[LAST_A : LAST_A + 1, :] = last


def kernel(pn, names, sens_hbm, bun_hbm, cel_hbm, state_hbm, prior_hbm, obs_hbm, wgt_hbm, new_ref, res_ref, *scratch):
    w = dict(zip(names, scratch))
    sens, state, prior = w["sens"], w["state"], w["prior"]
    tab, x1, res_t = w["tab"], w["x1"], w["res_t"]
    st_t, pr_t = w["st_t"], w["pr_t"]
    load_sem, send_sem, recv_sem = w["load_sem"], w["send_sem"], w["recv_sem"]
    nx, nz, ny, nblk, ncell, half, cown = pn.nx, pn.nz, pn.ny, pn.nblk, pn.ncell, pn.half, pn.cown

    s, b = lax.axis_index("shot"), lax.axis_index("band")
    y, core = s // 2, s % 2
    x, z = b // nz, b % nz
    size = {"x": nx, "y": ny, "z": nz, "core": 2}
    place = {"x": x, "y": y, "z": z, "core": core}

    def at(axis, k):
        return (place[axis] + k) % size[axis]

    def device(axis, k):
        if axis == "x":
            return {"band": at("x", k) * nz + z}
        if axis == "z":
            return {"band": x * nz + at("z", k)}
        if axis == "y":
            return {"shot": at("y", k) * 2 + core}
        return {"shot": y * 2 + (1 - core)}

    def order(axis):
        n = size[axis]
        return sorted(range(1, n), key=lambda k: -min(k, n - k))

    small = []
    for q, (src, name) in enumerate(((bun_hbm, "bun"), (cel_hbm, "cel"), (obs_hbm, "obs"), (wgt_hbm, "wgt"))):
        small.append(pltpu.make_async_copy(src, w[name], load_sem.at[4 + q]))
        small[-1].start()
    obs_ref, wgt_ref = w["obs"], w["wgt"]
    load_state = pltpu.make_async_copy(state_hbm, state, load_sem.at[0])
    load_prior = pltpu.make_async_copy(prior_hbm, prior, load_sem.at[1])
    load_sens = pltpu.make_async_copy(sens_hbm, sens, load_sem.at[2])
    load_state.start()
    load_prior.start()
    load_sens.start()

    barrier = pltpu.get_barrier_semaphore()
    greet = [(axis, k) for axis in ("z", "x", "y", "core") for k in order(axis)]
    for axis, k in greet:
        pl.semaphore_signal(barrier, inc=1, device_id=device(axis, k), device_id_type=MESH)

    for load in small:
        load.wait()
    index_table(w["bun"], w["cel"], w["pad"], w["table"], pn, x, z)
    to_smem = pltpu.make_async_copy(w["table"], tab, load_sem.at[3])
    to_smem.start()

    load_state.wait()
    load_prior.wait()

    def probe_block(i, carry):
        x1[i] = (state[i] + 0.5 * prior[i]).astype(BF16).T
        return carry

    lax.fori_loop(0, ncell, probe_block, 0, unroll=4)
    for g in range(len(pn.groups)):
        w[f"pref{g}"][nblk] = jnp.zeros(w[f"pref{g}"].shape[1:], F32)
    to_smem.wait()
    load_sens.wait()

    counter = [0]
    first_send = [True]

    class Exchange:
        def __init__(self, axis, out, came_all):
            self.axis, self.out, self.came_all = axis, out, came_all
            self.index = counter[0]
            counter[0] += 1
            if first_send[0]:
                first_send[0] = False
                pl.semaphore_wait(barrier, len(greet))

        def send(self, k, src, dst):
            pltpu.make_async_remote_copy(
                src_ref=src, dst_ref=dst, send_sem=send_sem.at[self.out], recv_sem=recv_sem.at[self.index],
                device_id=device(self.axis, k), device_id_type=MESH).start()

        def wait(self):
            pltpu.make_async_copy(self.came_all, self.came_all, recv_sem.at[self.index]).wait()

    def products(pref, m, order_row, keep_row, dims, field):
        def step(k, acc):
            prod = lax.dot_general(field(k), sens[tab[order_row, k]], dims, preferred_element_type=F32)
            acc = jnp.where(tab[keep_row, k] > 0, acc, 0.0) + prod
            pref[k] = acc
            return acc

        lax.fori_loop(0, nblk, step, jnp.zeros((m, T), F32), unroll=UNROLL)

    def group(g):
        row, parts = pn.groups[g]
        m = sum(rows for rows, _ in parts)
        starts = [sum(rows for rows, _ in parts[:u]) for u in range(len(parts))]
        pref, g1 = w[f"pref{g}"], w[f"g1_{g}"]
        span = slice(row, row + m)
        for p in range(2):
            out = 2 * g + p
            Q = w[f"Q{g}_{p}"]
            ys, yr = w[f"ys{g}_{p}"], w[f"yr{g}_{p}"]

            def field_f(k):
                i = tab[CEL_F, k]
                return x1[i, span, :] if p == 0 else w[f"Q{g}_0"][i]

            products(pref, m, ORD_F, KEEP_F, NT_DIMS, field_f)

            def part(u):
                rows, zfirst = parts[u]
                key = f"{g}_{p}_{u}"
                bsb, brb, own, R = (w[q + key] for q in ("bs", "br", "own", "R"))
                inner = slice(starts[u], starts[u] + rows)
                one, two = ("z", "x") if zfirst else ("x", "z")
                first, second = size[one], size[two]
                back = second // 4
                mine = place[one]

                def term(d, c):
                    bundle = c * nz + d if zfirst else d * nz + c
                    return pref[tab[LAST_F, bundle], inner, :]

                opened = []
                for q, (low, count) in reversed(list(enumerate(spans(second)))):
                    asb, arb = w[f"as{q}" + key], w[f"ar{q}" + key]
                    ex = Exchange(one, out, arb)
                    for k in order(one):
                        for j in range(count):
                            asb[k - 1, j] = term(at(one, k), at(two, low + j - back + second)).astype(BF16)
                        ex.send(k, asb.at[k - 1], arb.at[k - 1])
                    opened.append((ex, arb, low, count))
                yield
                across = Exchange(two, out, brb)
                for ex, arb, low, count in opened:
                    ex.wait()
                    for j in range(count):
                        k2 = (low + j - back) % second
                        total = term(mine, at(two, k2))
                        for k in range(1, first):
                            total = total + arb[k - 1, j].astype(F32)
                        if k2 == 0:
                            own[...] = total
                        else:
                            bsb[k2 - 1] = total.astype(BF16)
                            across.send(k2, bsb.at[k2 - 1], brb.at[k2 - 1])
                yield
                across.wait()
                pred = own[...]
                for k in range(1, second):
                    pred = pred + brb[k - 1].astype(F32)
                r = wgt_ref[...] * (pred - obs_ref[...])
                if p == 1:
                    res_t[row + starts[u] : row + starts[u] + rows, :] = r
                R[mine, back] = r.astype(BF16)
                opened = []
                for low, count in reversed(spans(second)):
                    steps = [(low + j - back) % second for j in range(count)]
                    steps = [k for k in steps if k]
                    every = R.at[0, pl.ds(0, len(steps))]
                    ex = Exchange(two, out, every)
                    for k in steps:
                        ex.send(k, R.at[mine, back], R.at[mine, (back - k) % second])
                    opened.append((ex, low, count))
                yield
                across = []
                for ex, low, count in reversed(opened):
                    ex.wait()
                    every = R.at[pl.ds(0, first - 1), pl.ds(0, count)]
                    spread = Exchange(one, out, every)
                    ref = R.at[mine, pl.ds(low, count)]
                    for k in order(one):
                        spread.send(k, ref, ref)
                    across.append(spread)
                yield
                for ex in across:
                    ex.wait()

            running = [part(u) for u in range(len(parts))]
            for _ in range(4):
                for q in running:
                    next(q)
                yield
            for q in running:
                for _ in q:
                    pass

            def field_a(k):
                pieces = []
                for u, (rows, zfirst) in enumerate(parts):
                    R = w[f"R{g}_{p}_{u}"]
                    pieces.append(R[tab[BZ_A, k], tab[RX_A, k]] if zfirst else R[tab[BX_A, k], tab[RZ_A, k]])
                return pieces[0] if len(pieces) == 1 else jnp.concatenate(pieces, axis=0)

            products(pref, m, ORD_A, KEEP_A, NN_DIMS, field_a)

            cs, cr = w[f"cs{g}_{p}"], w[f"cr{g}_{p}"]
            for i in range(half):
                cs[i] = pref[tab[LAST_A, (1 - core) * half + i]].astype(BF16)
            ex = Exchange("core", out, cr)
            ex.send(1, cs, cr)
            if g == 0 and p == 0:
                for c in range(cown):
                    st_t[c] = state[core * half + y * cown + c].T
                    pr_t[c] = prior[core * half + y * cown + c].T
            yield
            ex.wait()

            def grad_term(d, c):
                i = d * cown + c
                return pref[tab[LAST_A, core * half + i]] + cr[i].astype(F32)

            if ny > 1:
                ex = Exchange("y", out, yr)
                for k in order("y"):
                    for c in range(cown):
                        ys[k - 1, c] = grad_term(at("y", k), c).astype(BF16)
                    ex.send(k, ys.at[k - 1], yr.at[k - 1])
                yield
                ex.wait()
            base = core * half + y * cown
            for c in range(cown):
                grad = grad_term(y, c)
                for k in range(1, ny):
                    grad = grad + yr[k - 1, c].astype(F32)
                if p == 0:
                    g1[c] = grad
                    st, pr = st_t[c, span, :], pr_t[c, span, :]
                    middle = st + 0.5 * (pr - 0.5 * grad)
                    Q[base + c] = (middle + 0.5 * pr).astype(BF16)
                else:
                    Q[base + c] = (g1[c] + grad).astype(BF16)
            if ny > 1:
                rest = Q.at[pl.ds(0, (ny - 1) * cown)]
                ref = Q.at[pl.ds(base, cown)]
                ex = Exchange("y", out, rest)
                for k in order("y"):
                    ex.send(k, ref, ref)
                yield
                ex.wait()
            ref = Q.at[pl.ds(core * half, half)]
            ex = Exchange("core", out, ref)
            ex.send(1, ref, ref)
            if p == 1:
                last.append(ex)
                return
            yield
            ex.wait()

    last = []
    live = [(g * LAG, group(g)) for g in range(len(pn.groups))]
    tick = 0
    while live:
        for start, q in list(live):
            if tick >= start and next(q, "end") == "end":
                live.remove((start, q))
        tick += 1

    res_ref[0] = res_t[...].T

    def final_block(i, start):
        pieces = [w[f"Q{g}_1"][start + i].astype(F32) for g in range(len(pn.groups))]
        total = jnp.concatenate(pieces, axis=0).T
        new_ref[start + i] = state[start + i] + 0.5 * (prior[start + i] - 0.25 * total)
        return start

    lax.fori_loop(0, half, final_block, core * half, unroll=4)
    for ex in last:
        ex.wait()
    lax.fori_loop(0, half, final_block, (1 - core) * half, unroll=4)
    units = pn.nband - 1 + half + (ny - 1) * cown
    for g in range(len(pn.groups)):
        for p in range(2):
            every = w[f"pref{g}"].at[pl.ds(0, units)]
            pltpu.make_async_copy(every, every, send_sem.at[2 * g + p]).wait()


def per_device(pn, sensitivity, bundle_of, cellblock_of, state, prior_velocity, observed, pick_weight):
    ncell, nblk = pn.ncell, pn.nblk
    bufs = {
        "sens": ((nblk, T, T), BF16),
        "state": ((ncell, T, T), F32),
        "prior": ((ncell, T, T), F32),
        "x1": ((ncell, T, T), BF16),
        "res_t": ((T, T), F32),
        "st_t": ((pn.cown, T, T), F32),
        "pr_t": ((pn.cown, T, T), F32),
        "bun": ((nblk,), I32),
        "cel": ((nblk,), I32),
        "obs": ((1, T), F32),
        "wgt": ((1, T), F32),
        "pad": ((16, T), I32),
        "table": ((16, T), I32),
    }
    bufs.update(group_buffers(pn))
    shapes = {k: pltpu.VMEM(*v) for k, v in bufs.items()}
    shapes["tab"] = pltpu.SMEM((16, T), I32)
    shapes["load_sem"] = pltpu.SemaphoreType.DMA((8,))
    shapes["send_sem"] = pltpu.SemaphoreType.DMA((2 * len(pn.groups),))
    shapes["recv_sem"] = pltpu.SemaphoreType.DMA((pn.nsem,))
    hbm = pl.BlockSpec(memory_space=pltpu.HBM)
    vmem = pl.BlockSpec(memory_space=pltpu.VMEM)
    new_state, res = pl.pallas_call(
        functools.partial(kernel, pn, list(shapes)),
        out_shape=(
            jax.ShapeDtypeStruct((ncell, T, T), F32),
            jax.ShapeDtypeStruct((1, T, T), F32),
        ),
        in_specs=[hbm] * 7,
        out_specs=(vmem, vmem),
        scratch_shapes=list(shapes.values()),
        compiler_params=pltpu.CompilerParams(
            collective_id=0, has_side_effects=True, vmem_limit_bytes=VMEM_MB * 1024 * 1024),
        name="guided_update",
    )(sensitivity, bundle_of, cellblock_of, state.reshape(ncell, T, T), prior_velocity.reshape(ncell, T, T),
      observed, pick_weight)
    return new_state.reshape(ncell * T, T), res


def solution(mesh):
    nshot, nband = mesh.shape["shot"], mesh.shape["band"]
    in_specs = (
        P(("shot", "band"), None, None),
        P(("shot", "band")),
        P(("shot", "band")),
        P("band", None),
        P("band", None),
        P(("shot", "band"), None),
        P(("shot", "band"), None),
    )
    out_specs = (P("band", None), P(("shot", "band"), None, None))

    def body(sensitivity, bundle_of, cellblock_of, state, *rest):
        pn = Plan(nshot, nband, sensitivity.shape[0], state.shape[0] // T,
                  GROUPS)
        return per_device(pn, sensitivity, bundle_of, cellblock_of, state, *rest)

    return jax.shard_map(body, mesh=mesh, in_specs=in_specs, out_specs=out_specs, check_vma=False)
```

```python
import functools

import jax
import jax.numpy as jnp
from jax import lax
from jax.experimental import pallas as pl
from jax.experimental.pallas import tpu as pltpu
from jax.sharding import PartitionSpec as P

MESH = pl.DeviceIdType.MESH
BF16 = jnp.bfloat16
F32 = jnp.float32
I32 = jnp.int32
T = 128
NT_DIMS = (((1,), (1,)), ((), ()))
NN_DIMS = (((1,), (0,)), ((), ()))
UNROLL = 64
LAG = 0
VMEM_MB = 60
GROUPS = ((0, ((32, False),)), (32, ((16, True), (32, False))), (80, ((16, True), (32, False))))
ORD_F, CEL_F, KEEP_F, LAST_F, ORD_A, BX_A, BZ_A, KEEP_A, LAST_A, RX_A, RZ_A = range(11)


def band_grid(nband):
    nx = 4 if nband >= 16 else 2
    return nx, nband // nx


class Plan:
    def __init__(self, nshot, nband, nblk, ncell, groups):
        self.nx, self.nz = band_grid(nband)
        self.ny = nshot // 2
        self.nblk, self.ncell, self.nband = nblk, ncell, nband
        self.half = ncell // 2
        self.cown = ncell // nshot
        self.groups = groups
        self.nsem = len(groups) * 2 * 4 + sum(14 * len(parts) for _, parts in groups)


def spans(n):
    far = max(n // 2 - 1, 0)
    return [(0, n - far)] + ([(n - far, far)] if far else [])


def group_buffers(pn):
    bufs = {}
    for g, (row, parts) in enumerate(pn.groups):
        m = sum(rows for rows, _ in parts)
        bufs[f"pref{g}"] = ((pn.nblk + 1, m, T), F32)
        bufs[f"g1_{g}"] = ((pn.cown, m, T), F32)
        for p in range(2):
            bufs[f"Q{g}_{p}"] = ((pn.ncell, m, T), BF16)
            for d in "sr":
                bufs[f"c{d}{g}_{p}"] = ((pn.half, m, T), BF16)
                bufs[f"y{d}{g}_{p}"] = ((max(pn.ny - 1, 1), pn.cown, m, T), BF16)
            for u, (rows, zfirst) in enumerate(parts):
                first, second = (pn.nz, pn.nx) if zfirst else (pn.nx, pn.nz)
                k = f"{g}_{p}_{u}"
                bufs[f"own{k}"] = ((rows, T), F32)
                bufs[f"R{k}"] = ((first, second, rows, T), BF16)
                for d in "sr":
                    for q, (_, count) in enumerate(spans(second)):
                        bufs[f"a{d}{q}{k}"] = ((first - 1, count, rows, T), BF16)
                    bufs[f"b{d}{k}"] = ((second - 1, rows, T), BF16)
    return bufs


def index_table(bun_ref, cel_ref, pad_ref, table_ref, pn, x, z):
    n = pn.nblk
    lane = lax.broadcasted_iota(I32, (T, T), 1)
    sub = lax.broadcasted_iota(I32, (T, T), 0)
    pad_ref[...] = jnp.full(pad_ref.shape, 127, I32)
    pad_ref[0:1, 0:n] = bun_ref[...].reshape(1, n)
    pad_ref[8:9, 0:n] = cel_ref[...].reshape(1, n)
    b = jnp.broadcast_to(pad_ref[0:1, :], (T, T))
    c = jnp.broadcast_to(pad_ref[8:9, :], (T, T))

    def ranked(key, other):
        key_t = key.T
        before = (key_t < key) | ((key_t == key) & (sub < lane))
        rank = jnp.sum(before.astype(I32), axis=0, keepdims=True)
        same = jnp.sum(((key_t == key) & (sub < lane)).astype(I32), axis=0, keepdims=True)
        keep = (same > 0).astype(I32)
        packed = rank * 65536 + keep * 16384 + other[0:1, :] * 128 + lane[0:1, :]
        packed = jnp.broadcast_to(packed, (T, T)).T
        mine = (packed // 65536) == lane
        row = jnp.sum(jnp.where(mine, packed % 65536, 0), axis=0, keepdims=True)
        upto = jnp.sum((key_t <= lane).astype(I32), axis=0, keepdims=True)
        held = jnp.sum((key_t == lane).astype(I32), axis=0, keepdims=True)
        last = jnp.where(held > 0, upto - 1, n)
        return row % 128, (row // 128) % 128, row // 16384, last

    order, other, keep, last = ranked(b, c)
    table_ref[ORD_F : ORD_F + 1, :] = order
    table_ref[CEL_F : CEL_F + 1, :] = other
    table_ref[KEEP_F : KEEP_F + 1, :] = keep
    table_ref[LAST_F : LAST_F + 1, :] = last
    order, other, keep, last = ranked(c, b)
    table_ref[ORD_A : ORD_A + 1, :] = order
    table_ref[BX_A : BX_A + 1, :] = other // pn.nz
    table_ref[BZ_A : BZ_A + 1, :] = other % pn.nz
    table_ref[RX_A : RX_A + 1, :] = (other // pn.nz + (pn.nx + pn.nx // 4 - x)) % pn.nx
    table_ref[RZ_A : RZ_A + 1, :] = (other % pn.nz + (pn.nz + pn.nz // 4 - z)) % pn.nz
    table_ref[KEEP_A : KEEP_A + 1, :] = keep
    table_ref[LAST_A : LAST_A + 1, :] = last


def kernel(pn, names, sens_hbm, bun_hbm, cel_hbm, state_hbm, prior_hbm, obs_hbm, wgt_hbm, new_ref, res_ref, *scratch):
    w = dict(zip(names, scratch))
    sens, state, prior = w["sens"], w["state"], w["prior"]
    tab, x1, res_t = w["tab"], w["x1"], w["res_t"]
    st_t, pr_t = w["st_t"], w["pr_t"]
    load_sem, send_sem, recv_sem = w["load_sem"], w["send_sem"], w["recv_sem"]
    nx, nz, ny, nblk, ncell, half, cown = pn.nx, pn.nz, pn.ny, pn.nblk, pn.ncell, pn.half, pn.cown

    s, b = lax.axis_index("shot"), lax.axis_index("band")
    y, core = s // 2, s % 2
    x, z = b // nz, b % nz
    size = {"x": nx, "y": ny, "z": nz, "core": 2}
    place = {"x": x, "y": y, "z": z, "core": core}

    def at(axis, k):
        return (place[axis] + k) % size[axis]

    def device(axis, k):
        if axis == "x":
            return {"band": at("x", k) * nz + z}
        if axis == "z":
            return {"band": x * nz + at("z", k)}
        if axis == "y":
            return {"shot": at("y", k) * 2 + core}
        return {"shot": y * 2 + (1 - core)}

    def order(axis):
        n = size[axis]
        return sorted(range(1, n), key=lambda k: -min(k, n - k))

    small = []
    for q, (src, name) in enumerate(((bun_hbm, "bun"), (cel_hbm, "cel"), (obs_hbm, "obs"), (wgt_hbm, "wgt"))):
        small.append(pltpu.make_async_copy(src, w[name], load_sem.at[4 + q]))
        small[-1].start()
    obs_ref, wgt_ref = w["obs"], w["wgt"]
    load_state = pltpu.make_async_copy(state_hbm, state, load_sem.at[0])
    load_prior = pltpu.make_async_copy(prior_hbm, prior, load_sem.at[1])
    load_sens = pltpu.make_async_copy(sens_hbm, sens, load_sem.at[2])
    load_state.start()
    load_prior.start()
    load_sens.start()

    barrier = pltpu.get_barrier_semaphore()
    greet = [(axis, k) for axis in ("z", "x", "y", "core") for k in order(axis)]
    for axis, k in greet:
        pl.semaphore_signal(barrier, inc=1, device_id=device(axis, k), device_id_type=MESH)

    for load in small:
        load.wait()
    index_table(w["bun"], w["cel"], w["pad"], w["table"], pn, x, z)
    to_smem = pltpu.make_async_copy(w["table"], tab, load_sem.at[3])
    to_smem.start()

    load_state.wait()
    load_prior.wait()

    def probe_block(i, carry):
        x1[i] = (state[i] + 0.5 * prior[i]).astype(BF16).T
        return carry

    lax.fori_loop(0, ncell, probe_block, 0, unroll=4)
    for g in range(len(pn.groups)):
        w[f"pref{g}"][nblk] = jnp.zeros(w[f"pref{g}"].shape[1:], F32)
    to_smem.wait()
    load_sens.wait()

    counter = [0]
    first_send = [True]

    class Exchange:
        def __init__(self, axis, out, came_all):
            self.axis, self.out, self.came_all = axis, out, came_all
            self.index = counter[0] % (pn.nsem // 2)
            counter[0] += 1
            if first_send[0]:
                first_send[0] = False
                pl.semaphore_wait(barrier, len(greet))

        def send(self, k, src, dst):
            pltpu.make_async_remote_copy(
                src_ref=src, dst_ref=dst, send_sem=send_sem.at[self.out], recv_sem=recv_sem.at[self.index],
                device_id=device(self.axis, k), device_id_type=MESH).start()

        def wait(self):
            pltpu.make_async_copy(self.came_all, self.came_all, recv_sem.at[self.index]).wait()

    def products(pref, m, order_row, keep_row, dims, field):
        def step(k, acc):
            prod = lax.dot_general(field(k), sens[tab[order_row, k]], dims, preferred_element_type=F32)
            acc = jnp.where(tab[keep_row, k] > 0, acc, 0.0) + prod
            pref[k] = acc
            return acc

        lax.fori_loop(0, nblk, step, jnp.zeros((m, T), F32), unroll=UNROLL)

    def group(g):
        row, parts = pn.groups[g]
        m = sum(rows for rows, _ in parts)
        starts = [sum(rows for rows, _ in parts[:u]) for u in range(len(parts))]
        pref, g1 = w[f"pref{g}"], w[f"g1_{g}"]
        span = slice(row, row + m)
        for p in range(2):
            out = 2 * g + p
            Q = w[f"Q{g}_{p}"]
            ys, yr = w[f"ys{g}_{p}"], w[f"yr{g}_{p}"]

            def field_f(k):
                i = tab[CEL_F, k]
                return x1[i, span, :] if p == 0 else w[f"Q{g}_0"][i]

            products(pref, m, ORD_F, KEEP_F, NT_DIMS, field_f)

            def part(u):
                rows, zfirst = parts[u]
                key = f"{g}_{p}_{u}"
                bsb, brb, own, R = (w[q + key] for q in ("bs", "br", "own", "R"))
                inner = slice(starts[u], starts[u] + rows)
                one, two = ("z", "x") if zfirst else ("x", "z")
                first, second = size[one], size[two]
                back = second // 4
                mine = place[one]

                def term(d, c):
                    bundle = c * nz + d if zfirst else d * nz + c
                    return pref[tab[LAST_F, bundle], inner, :]

                opened = []
                for q, (low, count) in reversed(list(enumerate(spans(second)))):
                    asb, arb = w[f"as{q}" + key], w[f"ar{q}" + key]
                    ex = Exchange(one, out, arb)
                    for k in order(one):
                        for j in range(count):
                            asb[k - 1, j] = term(at(one, k), at(two, low + j - back + second)).astype(BF16)
                        ex.send(k, asb.at[k - 1], arb.at[k - 1])
                    opened.append((ex, arb, low, count))
                yield
                across = Exchange(two, out, brb)
                for ex, arb, low, count in opened:
                    ex.wait()
                    for j in range(count):
                        k2 = (low + j - back) % second
                        total = term(mine, at(two, k2))
                        for k in range(1, first):
                            total = total + arb[k - 1, j].astype(F32)
                        if k2 == 0:
                            own[...] = total
                        else:
                            bsb[k2 - 1] = total.astype(BF16)
                            across.send(k2, bsb.at[k2 - 1], brb.at[k2 - 1])
                yield
                across.wait()
                pred = own[...]
                for k in range(1, second):
                    pred = pred + brb[k - 1].astype(F32)
                r = wgt_ref[...] * (pred - obs_ref[...])
                if p == 1:
                    res_t[row + starts[u] : row + starts[u] + rows, :] = r
                R[mine, back] = r.astype(BF16)
                opened = []
                for low, count in reversed(spans(second)):
                    steps = [(low + j - back) % second for j in range(count)]
                    steps = [k for k in steps if k]
                    every = R.at[0, pl.ds(0, len(steps))]
                    ex = Exchange(two, out, every)
                    for k in steps:
                        ex.send(k, R.at[mine, back], R.at[mine, (back - k) % second])
                    opened.append((ex, low, count))
                yield
                across = []
                for ex, low, count in reversed(opened):
                    ex.wait()
                    every = R.at[pl.ds(0, first - 1), pl.ds(0, count)]
                    spread = Exchange(one, out, every)
                    ref = R.at[mine, pl.ds(low, count)]
                    for k in order(one):
                        spread.send(k, ref, ref)
                    across.append(spread)
                yield
                for ex in across:
                    ex.wait()

            running = [part(u) for u in range(len(parts))]
            for _ in range(4):
                for q in running:
                    next(q)
                yield
            for q in running:
                for _ in q:
                    pass

            def field_a(k):
                pieces = []
                for u, (rows, zfirst) in enumerate(parts):
                    R = w[f"R{g}_{p}_{u}"]
                    pieces.append(R[tab[BZ_A, k], tab[RX_A, k]] if zfirst else R[tab[BX_A, k], tab[RZ_A, k]])
                return pieces[0] if len(pieces) == 1 else jnp.concatenate(pieces, axis=0)

            products(pref, m, ORD_A, KEEP_A, NN_DIMS, field_a)

            cs, cr = w[f"cs{g}_{p}"], w[f"cr{g}_{p}"]
            for i in range(half):
                cs[i] = pref[tab[LAST_A, (1 - core) * half + i]].astype(BF16)
            ex = Exchange("core", out, cr)
            ex.send(1, cs, cr)
            if g == 0 and p == 0:
                for c in range(cown):
                    st_t[c] = state[core * half + y * cown + c].T
                    pr_t[c] = prior[core * half + y * cown + c].T
            yield
            ex.wait()

            def grad_term(d, c):
                i = d * cown + c
                return pref[tab[LAST_A, core * half + i]] + cr[i].astype(F32)

            if ny > 1:
                ex = Exchange("y", out, yr)
                for k in order("y"):
                    for c in range(cown):
                        ys[k - 1, c] = grad_term(at("y", k), c).astype(BF16)
                    ex.send(k, ys.at[k - 1], yr.at[k - 1])
                yield
                ex.wait()
            base = core * half + y * cown
            for c in range(cown):
                grad = grad_term(y, c)
                for k in range(1, ny):
                    grad = grad + yr[k - 1, c].astype(F32)
                if p == 0:
                    g1[c] = grad
                    st, pr = st_t[c, span, :], pr_t[c, span, :]
                    middle = st + 0.5 * (pr - 0.5 * grad)
                    Q[base + c] = (middle + 0.5 * pr).astype(BF16)
                else:
                    Q[base + c] = (g1[c] + grad).astype(BF16)
            if ny > 1:
                rest = Q.at[pl.ds(0, (ny - 1) * cown)]
                ref = Q.at[pl.ds(base, cown)]
                ex = Exchange("y", out, rest)
                for k in order("y"):
                    ex.send(k, ref, ref)
                yield
                ex.wait()
            ref = Q.at[pl.ds(core * half, half)]
            ex = Exchange("core", out, ref)
            ex.send(1, ref, ref)
            if p == 1:
                last.append(ex)
                return
            yield
            ex.wait()

    last = []
    live = [(g * LAG, group(g)) for g in range(len(pn.groups))]
    tick = 0
    while live:
        for start, q in list(live):
            if tick >= start and next(q, "end") == "end":
                live.remove((start, q))
        tick += 1

    res_ref[0] = res_t[...].T

    def final_block(i, start):
        pieces = [w[f"Q{g}_1"][start + i].astype(F32) for g in range(len(pn.groups))]
        total = jnp.concatenate(pieces, axis=0).T
        new_ref[start + i] = state[start + i] + 0.5 * (prior[start + i] - 0.25 * total)
        return start

    lax.fori_loop(0, half, final_block, core * half, unroll=4)
    for ex in last:
        ex.wait()
    lax.fori_loop(0, half, final_block, (1 - core) * half, unroll=4)
    units = pn.nband - 1 + half + (ny - 1) * cown
    for g in range(len(pn.groups)):
        for p in range(2):
            every = w[f"pref{g}"].at[pl.ds(0, units)]
            pltpu.make_async_copy(every, every, send_sem.at[2 * g + p]).wait()


def per_device(pn, sensitivity, bundle_of, cellblock_of, state, prior_velocity, observed, pick_weight):
    ncell, nblk = pn.ncell, pn.nblk
    bufs = {
        "sens": ((nblk, T, T), BF16),
        "state": ((ncell, T, T), F32),
        "prior": ((ncell, T, T), F32),
        "x1": ((ncell, T, T), BF16),
        "res_t": ((T, T), F32),
        "st_t": ((pn.cown, T, T), F32),
        "pr_t": ((pn.cown, T, T), F32),
        "bun": ((nblk,), I32),
        "cel": ((nblk,), I32),
        "obs": ((1, T), F32),
        "wgt": ((1, T), F32),
        "pad": ((16, T), I32),
        "table": ((16, T), I32),
    }
    bufs.update(group_buffers(pn))
    shapes = {k: pltpu.VMEM(*v) for k, v in bufs.items()}
    shapes["tab"] = pltpu.SMEM((16, T), I32)
    shapes["load_sem"] = pltpu.SemaphoreType.DMA((8,))
    shapes["send_sem"] = pltpu.SemaphoreType.DMA((2 * len(pn.groups),))
    shapes["recv_sem"] = pltpu.SemaphoreType.DMA((pn.nsem // 2,))
    hbm = pl.BlockSpec(memory_space=pltpu.HBM)
    vmem = pl.BlockSpec(memory_space=pltpu.VMEM)
    new_state, res = pl.pallas_call(
        functools.partial(kernel, pn, list(shapes)),
        out_shape=(
            jax.ShapeDtypeStruct((ncell, T, T), F32),
            jax.ShapeDtypeStruct((1, T, T), F32),
        ),
        in_specs=[hbm] * 7,
        out_specs=(vmem, vmem),
        scratch_shapes=list(shapes.values()),
        compiler_params=pltpu.CompilerParams(
            collective_id=0, has_side_effects=True, vmem_limit_bytes=VMEM_MB * 1024 * 1024),
        name="guided_update",
    )(sensitivity, bundle_of, cellblock_of, state.reshape(ncell, T, T), prior_velocity.reshape(ncell, T, T),
      observed, pick_weight)
    return new_state.reshape(ncell * T, T), res


def solution(mesh):
    nshot, nband = mesh.shape["shot"], mesh.shape["band"]
    in_specs = (
        P(("shot", "band"), None, None),
        P(("shot", "band")),
        P(("shot", "band")),
        P("band", None),
        P("band", None),
        P(("shot", "band"), None),
        P(("shot", "band"), None),
    )
    out_specs = (P("band", None), P(("shot", "band"), None, None))

    def body(sensitivity, bundle_of, cellblock_of, state, *rest):
        pn = Plan(nshot, nband, sensitivity.shape[0], state.shape[0] // T,
                  GROUPS)
        return per_device(pn, sensitivity, bundle_of, cellblock_of, state, *rest)

    return jax.shard_map(body, mesh=mesh, in_specs=in_specs, out_specs=out_specs, check_vma=False)
```
